128 devices in a mesh: ctx: 16 (over y_lo, x, core), tp: 8 (over z, y_hi).
Axes of the slice: x: 4, y: 4 (y_hi: 2, y_lo: 2; y = y_hi * 2 + y_lo), z: 4, core: 2. Of those that a mesh axis runs over, the one named last changes fastest.
Arguments:
- hidden_in: bfloat16 [16384, 4096], P(('ctx', 'tp')), may hold values from -6 to 6
- gain: bfloat16 [4096], replicated, may hold values from 0.5 to 1.5
- positions: int32 [16384], P('ctx'), may hold values from 0 to 16383, as said below
- w_query: bfloat16 [4096, 4096], P(None, 'tp')
- w_key: bfloat16 [4096, 1024], P(None, 'tp')
- w_value: bfloat16 [4096, 1024], P(None, 'tp'), may hold values from -0.09375 to 0.09375
- w_out: bfloat16 [4096, 4096], P('tp'), may hold values from -0.09375 to 0.09375
Outputs:
- hidden_out: bfloat16 [16384, 4096], P(('ctx', 'tp'))
The draws below stay inside these ranges and needn't reach their ends.
Inputs may be any that keep to these rules, and one draw needn't show every extreme that they name: A permutation of 0 to 16383. The 1024 rows of one index of ctx hold two blocks of 512 consecutive positions in rising order: block c, then block 31 - c, for some c; which c lies on which index is drawn.
All inputs are finite; a program needn't handle non-finite values.
Results may differ from the reference program's by a relative error of at most 0.015.
The reference program's roundings to bfloat16 on the way count: a program that leaves them out, or rounds other values in their place, can miss the bound.
Values may be sent and summed in bfloat16 or wider, within the bound.
No kernel may reach another device: no remote copies, remote signals or barrier semaphores. Data moves between devices by JAX's collectives and lax.ppermute only.
A program may use at most 128 MiB of HBM per device.

```python
import jax
import jax.numpy as jnp
from jax import lax

D = 4096
QH = 32
KVH = 8
HEAD = 128
SPAN = 512
SEQ = 16384
N_CTX = 16
N_TP = 8


def query_base(key):
    return jax.random.normal(key, (D, QH * HEAD), jnp.float32) * D ** (-0.5)


def draw_w_query(key, part):
    base = query_base(key)
    return base.astype(jnp.bfloat16)


def draw_w_key(key, part):
    key = jax.random.fold_in(key, 3)
    noise = jax.random.normal(key, (D, KVH * HEAD), jnp.float32) * D ** (-0.5)
    return noise.astype(jnp.bfloat16)


def draw_positions(key, part):
    key = jax.random.fold_in(key, 7)
    order = jax.random.permutation(key, N_CTX).astype(jnp.int32)
    within = jnp.arange(SPAN, dtype=jnp.int32)
    first = order[:, None] * SPAN + within[None, :]
    second = (2 * N_CTX - 1 - order)[:, None] * SPAN + within[None, :]
    return jnp.concatenate([first, second], axis=1).reshape(-1).astype(jnp.int32)


def steps_of(own_key, dims, shards, low, top_value):
    loudness, own = 1.0, jax.random.fold_in(own_key, 6)
    for position, blocks in shards:
        heights = jnp.exp(jax.random.uniform(jax.random.fold_in(own, position), (blocks,), jnp.float32, low / len(shards), top_value / len(shards)))
        loudness = loudness * jnp.repeat(heights, dims[position] // blocks).reshape([-1 if axis == position else 1 for axis in range(len(dims))])
    return loudness


def scatter_about(rng, extent, scale, limit, split=(), kind=jnp.bfloat16):
    entries = jax.random.normal(rng, extent, jnp.float32) * scale
    if len(split) > 0:
        entries = steps_of(rng, extent, split, -0.22, 0.18) * entries
    return jnp.clip(entries, min=-limit, max=limit).astype(kind)


def setup_inputs(seed: int = 0) -> dict:
    key_of = jax.random.split(jax.random.key(seed), 8)
    hidden_in = scatter_about(key_of[0], (SEQ, D), 1.0, 6.0, ((0, 128),))
    gain = jnp.clip(1.0 + 0.1 * jax.random.normal(key_of[1], (D,), jnp.float32), 0.5, 1.5).astype(jnp.bfloat16)
    positions = draw_positions(jax.random.fold_in(key_of[7], 71), 0)
    w_query = draw_w_query(jax.random.fold_in(key_of[7], 71), 0)
    w_key = draw_w_key(jax.random.fold_in(key_of[7], 71), 0)
    w_value = scatter_about(key_of[5], (D, KVH * HEAD), D ** -0.5, 0.09375, ((1, 8),))
    w_out = scatter_about(key_of[6], (QH * HEAD, D), (QH * HEAD) ** -0.5, 0.09375, ((0, 8),))
    return dict(hidden_in=hidden_in, gain=gain, positions=positions, w_query=w_query, w_key=w_key, w_value=w_value, w_out=w_out)


EPS = 1e-05
BASE = 500000.0

def rope_angles(positions, head):
    half = head // 2
    freq = BASE ** (-(jnp.arange(half, dtype=jnp.float32) * 2.0 / head))
    angle = positions.astype(jnp.float32)[:, None] * freq[None, :]
    return (jnp.cos(angle), jnp.sin(angle))

def rotate(vectors, cosine, sine):
    half = vectors.shape[-1] // 2
    first = vectors[..., :half]
    second = vectors[..., half:]
    cosine = cosine[:, None, :]
    sine = sine[:, None, :]
    return jnp.concatenate([first * cosine - second * sine, second * cosine + first * sine], axis=-1)

def reference(hidden_in, gain, positions, w_query, w_key, w_value, w_out):
    widened = hidden_in.astype(jnp.float32)
    scale_rows = lax.rsqrt(lax.optimization_barrier(jnp.mean(widened * widened, axis=-1, keepdims=True)) + EPS)
    normed = (widened * scale_rows * gain.astype(jnp.float32)).astype(jnp.bfloat16)
    count_rows = normed.shape[0]
    cosine, sine = rope_angles(positions, HEAD)
    query = jnp.dot(normed, w_query, preferred_element_type=jnp.float32).reshape(count_rows, QH, HEAD)
    query = rotate(query, cosine, sine).astype(jnp.bfloat16)
    keys = jnp.dot(normed, w_key, preferred_element_type=jnp.float32).reshape(count_rows, KVH, HEAD)
    keys = rotate(keys, cosine, sine).astype(jnp.bfloat16)
    values = jnp.dot(normed, w_value, preferred_element_type=jnp.float32).astype(jnp.bfloat16)
    values = values.reshape(count_rows, KVH, HEAD)
    allowed = positions[:, None] >= positions[None, :]
    group = QH // KVH
    score_scale = 1.0 / HEAD ** 0.5

    def one_head(index):
        query_head = lax.dynamic_index_in_dim(query, index, 1, keepdims=False)
        key_head = lax.dynamic_index_in_dim(keys, index // group, 1, keepdims=False)
        value_head = lax.dynamic_index_in_dim(values, index // group, 1, keepdims=False)
        scores = jnp.dot(query_head, key_head.T, preferred_element_type=jnp.float32) * score_scale
        scores = jnp.where(allowed, scores, -jnp.inf)
        largest = lax.optimization_barrier(jnp.max(scores, axis=-1, keepdims=True))
        weights = jnp.where(allowed, jnp.exp(scores - largest), 0.0)
        total = lax.optimization_barrier(jnp.sum(weights, axis=-1, keepdims=True))
        mixed = jnp.dot(weights.astype(jnp.bfloat16), value_head, preferred_element_type=jnp.float32) / total
        return mixed.astype(jnp.bfloat16)
    heads = lax.map(one_head, jnp.arange(QH, dtype=jnp.int32))
    mixed = jnp.transpose(heads, (1, 0, 2)).reshape(count_rows, QH * HEAD)
    width = QH * HEAD // N_TP

    def add_group(running, index):
        start = (index * width).astype(jnp.int32)
        part = lax.dynamic_slice_in_dim(mixed, start, width, 1)
        rows_out = lax.dynamic_slice_in_dim(w_out, start, width, 0)
        term = jnp.dot(part, rows_out, preferred_element_type=jnp.float32).astype(jnp.bfloat16)
        term = lax.optimization_barrier(term).astype(jnp.float32)
        return (running + term, None)
    summed, _ = lax.scan(add_group, jnp.zeros((count_rows, D), jnp.float32), jnp.arange(N_TP, dtype=jnp.int32))
    return (widened + summed).astype(jnp.bfloat16)
```

```python
import functools
import math

import jax
import jax.numpy as jnp
from jax import lax
from jax.experimental import pallas as pl
from jax.experimental.pallas import tpu as pltpu
from jax.sharding import Mesh
from jax.sharding import PartitionSpec as P

HEAD = 128
SPAN = 512
EPS = 1e-05
BASE = 500000.0
NEGATIVE = -1e30
PARTS = 2
VMEM_LIMIT = 56 * 2**20
SCORE_SCALE = math.log2(math.e) / HEAD**0.5


def rope_tables(positions):
    half = HEAD // 2
    freq = BASE ** (-(jnp.arange(half, dtype=jnp.float32) * 2.0 / HEAD))
    angle = positions.astype(jnp.float32)[:, None] * freq[None, :]
    cosine, sine = jnp.cos(angle), jnp.sin(angle)
    return (
        jnp.concatenate([cosine, cosine], axis=1),
        jnp.concatenate([-sine, sine], axis=1),
    )


def project_kernel(x_ref, wq_ref, wk_ref, wv_ref, cos_ref, sin_ref, q_ref, kv_ref):
    x = x_ref[...]
    cosine, sine = cos_ref[...], sin_ref[...]
    rows = x.shape[0]
    owned = HEAD
    piece = owned // PARTS

    def rope(u):
        return u * cosine + pltpu.roll(u, HEAD // 2, 1) * sine

    keys = jnp.dot(x, wk_ref[...], preferred_element_type=jnp.float32)
    kv_ref[:, :HEAD] = rope(keys).astype(jnp.bfloat16)
    values = jnp.dot(x, wv_ref[...], preferred_element_type=jnp.float32)
    kv_ref[:, HEAD:] = values.astype(jnp.bfloat16)
    query = jnp.dot(x, wq_ref[...], preferred_element_type=jnp.float32)
    for h in range(query.shape[1] // HEAD):
        turned = rope(query[:, h * HEAD : (h + 1) * HEAD]) * SCORE_SCALE
        turned = turned.astype(jnp.bfloat16)
        for t in range(rows // owned):
            for part in range(PARTS):
                start = t * owned + part * piece
                q_ref[part, 0, h, t * piece : (t + 1) * piece, :] = turned[
                    start : start + piece
                ]


def project(x, w_query, w_key, w_value, cosine, sine):
    count, width = x.shape
    step = 256
    heads = w_query.shape[1] // HEAD
    per_span = SPAN // step
    whole = lambda i: (0, 0)
    by_row = lambda i: (i, 0)
    flops = 2 * count * width * (w_query.shape[1] + 2 * HEAD)
    moved = 2 * (x.size + w_query.size + w_key.size + w_value.size)
    return pl.pallas_call(
        project_kernel,
        grid=(count // step,),
        in_specs=[
            pl.BlockSpec((step, width), by_row),
            pl.BlockSpec(w_query.shape, whole),
            pl.BlockSpec(w_key.shape, whole),
            pl.BlockSpec(w_value.shape, whole),
            pl.BlockSpec((step, HEAD), by_row),
            pl.BlockSpec((step, HEAD), by_row),
        ],
        out_specs=[
            pl.BlockSpec(
                (PARTS, 1, heads, step // PARTS, HEAD),
                lambda i: (0, i // per_span, 0, i % per_span, 0),
            ),
            pl.BlockSpec((step, 2 * HEAD), by_row),
        ],
        out_shape=[
            jax.ShapeDtypeStruct(
                (PARTS, count // SPAN, heads, SPAN // PARTS, HEAD), jnp.bfloat16
            ),
            jax.ShapeDtypeStruct((count, 2 * HEAD), jnp.bfloat16),
        ],
        compiler_params=pltpu.CompilerParams(vmem_limit_bytes=VMEM_LIMIT),
        cost_estimate=pl.CostEstimate(
            flops=flops, bytes_accessed=moved, transcendentals=0
        ),
    )(x, w_query, w_key, w_value, cosine, sine)


def attend_kernel(
    ids_ref, off_ref, q_ref, kv_ref, o_ref, max_ref, sum_ref, acc_ref,
    *, part, heads, pairs, key_step, row_step, unroll,
):
    per = q_ref.shape[0] // 2
    rows = per // heads
    piece = HEAD // PARTS

    def pair(which, block, masked):
        start = off_ref[block]
        for n in range(SPAN // key_step):
            at = pl.multiple_of(start + n * key_step, key_step)
            keys = kv_ref[pl.ds(at, key_step), :HEAD]
            values = kv_ref[pl.ds(at, key_step), HEAD:]
            for t in range(per // row_step):
                here = pl.ds(pl.multiple_of(which * per + t * row_step, row_step), row_step)
                scores = lax.dot_general(
                    q_ref[here, :], keys, (((1,), (1,)), ((), ())),
                    preferred_element_type=jnp.float32,
                )
                if masked:
                    row = lax.broadcasted_iota(jnp.int32, scores.shape, 0) & (rows - 1)
                    row = (row // piece) * HEAD + part * piece + (row & (piece - 1))
                    col = lax.broadcasted_iota(jnp.int32, scores.shape, 1) + n * key_step
                    scores = jnp.where(row >= col, scores, NEGATIVE)
                old = max_ref[here, :]
                new = jnp.maximum(old, jnp.max(scores, axis=1, keepdims=True))
                fade = jnp.exp2(old - new)
                weights = jnp.exp2(scores - jnp.concatenate([new] * (key_step // HEAD), axis=1))
                max_ref[here, :] = new
                added = weights[:, :HEAD]
                for u in range(1, key_step // HEAD):
                    added = added + weights[:, u * HEAD : (u + 1) * HEAD]
                sum_ref[here, :] = sum_ref[here, :] * fade + added
                acc_ref[here, :] = acc_ref[here, :] * fade + jnp.dot(
                    weights.astype(jnp.bfloat16), values, preferred_element_type=jnp.float32
                )

    max_ref[...] = jnp.full_like(max_ref, NEGATIVE)
    sum_ref[...] = jnp.zeros_like(sum_ref)
    acc_ref[...] = jnp.zeros_like(acc_ref)
    first = ids_ref[0]

    def plain(i):
        which = (i >= first).astype(jnp.int32)
        pair(which, i - which * first, False)

    def body(j, carry):
        for u in range(unroll):
            plain(j * unroll + u)
        return carry

    lax.fori_loop(0, pairs // unroll, body, 0)
    for i in range(pairs // unroll * unroll, pairs):
        plain(jnp.int32(i))
    for which in range(2):
        pair(which, ids_ref[which], True)
    for which in range(2):
        for h in range(heads):
            here = slice(which * per + h * rows, which * per + (h + 1) * rows)
            total = jnp.sum(sum_ref[here, :], axis=1, keepdims=True)
            o_ref[which * rows : (which + 1) * rows, h * HEAD : (h + 1) * HEAD] = (
                acc_ref[here, :] / total
            ).astype(jnp.bfloat16)


def attend(ids, offsets, query, kv, part):
    blocks, heads, rows, _ = query.shape
    pairs = kv.shape[0] // SPAN - 1
    query = query.reshape(blocks * heads * rows, HEAD)
    vmem = pl.BlockSpec(memory_space=pltpu.VMEM)
    smem = pl.BlockSpec(memory_space=pltpu.SMEM)
    scores = (pairs + 2) * heads * rows * SPAN
    return pl.pallas_call(
        functools.partial(
            attend_kernel, part=part, heads=heads, pairs=pairs,
            key_step=256, row_step=512, unroll=8,
        ),
        in_specs=[smem, smem, vmem, vmem],
        out_specs=vmem,
        out_shape=jax.ShapeDtypeStruct((blocks * rows, heads * HEAD), jnp.bfloat16),
        scratch_shapes=[pltpu.VMEM((blocks * heads * rows, HEAD), jnp.float32)] * 3,
        compiler_params=pltpu.CompilerParams(vmem_limit_bytes=VMEM_LIMIT),
        cost_estimate=pl.CostEstimate(
            flops=scores * HEAD * 8, bytes_accessed=2 * kv.size, transcendentals=scores
        ),
    )(ids, offsets, query, kv)


def per_device(hidden_in, gain, positions, w_query, w_key, w_value, w_out, *, n_ctx):
    widened = hidden_in.astype(jnp.float32)
    scale_rows = lax.rsqrt(jnp.mean(widened * widened, axis=-1, keepdims=True) + EPS)
    normed = (widened * scale_rows * gain.astype(jnp.float32)).astype(jnp.bfloat16)
    piece = lax.all_gather(normed, "tp", axis=0, tiled=True)
    cosine, sine = rope_tables(positions)

    ids = positions[::SPAN] // SPAN
    known = ids
    reach = 1
    while reach < n_ctx:
        shift = [(i, (i + reach) % n_ctx) for i in range(n_ctx)]
        known = jnp.concatenate([known, lax.ppermute(known, "ctx", shift)])
        reach *= 2
    owner = (lax.axis_index("ctx") - jnp.arange(n_ctx, dtype=jnp.int32)) % n_ctx
    at = (owner[:, None] * 2 + jnp.arange(2, dtype=jnp.int32)[None, :]).reshape(-1) * SPAN
    slots = jnp.arange(2 * n_ctx, dtype=jnp.int32)
    offsets = jnp.sum(jnp.where(known[:, None] == slots[None, :], at[:, None], 0), axis=0)

    piece, cosine, sine, offsets = lax.optimization_barrier((piece, cosine, sine, offsets))
    query, kv = project(piece, w_query, w_key, w_value, cosine, sine)
    kv = lax.all_gather(kv, "ctx", axis=0, tiled=True)
    terms = []
    for part in range(PARTS):
        mixed = attend(ids, offsets, query[part], kv, part)
        term = jnp.dot(mixed, w_out, preferred_element_type=jnp.float32).astype(jnp.bfloat16)
        terms.append(lax.psum_scatter(term, "tp", scatter_dimension=0, tiled=True))
    summed = jnp.concatenate(terms, axis=0).astype(jnp.float32)
    return (widened + summed).astype(jnp.bfloat16)


def solution(mesh):
    rows = P(("ctx", "tp"), None)
    in_specs = (
        rows, P(), P("ctx"), P(None, "tp"), P(None, "tp"), P(None, "tp"), P("tp", None),
    )
    return jax.shard_map(
        functools.partial(per_device, n_ctx=mesh.shape["ctx"]),
        mesh=mesh, in_specs=in_specs, out_specs=rows, check_vma=False,
    )
```

```python
import functools
import math

import jax
import jax.numpy as jnp
from jax import lax
from jax.experimental import pallas as pl
from jax.experimental.pallas import tpu as pltpu
from jax.sharding import Mesh
from jax.sharding import PartitionSpec as P

HEAD = 128
SPAN = 512
OWNED = 128
EPS = 1e-05
BASE = 500000.0
NEGATIVE = -1e30
PARTS = 2
PIECE = OWNED // PARTS
DIRECT = 64
TAIL = 16
VMEM_LIMIT = 56 * 2**20
SCORE_SCALE = math.log2(math.e) / HEAD**0.5

AXES = ("y_lo", "x", "core", "z", "y_hi")
CTX = AXES[:3]


def turn(x, by):
    return lax.ppermute(x, "z", [(i, (i + by) % 4) for i in range(4)])


def swap(x):
    return lax.ppermute(x, "y_hi", [(0, 1), (1, 0)])


def rope_tables(positions):
    half = HEAD // 2
    freq = BASE ** (-(jnp.arange(half, dtype=jnp.float32) * 2.0 / HEAD))
    angle = positions.astype(jnp.float32)[:, None] * freq[None, :]
    cosine, sine = jnp.cos(angle), jnp.sin(angle)
    return (
        jnp.concatenate([cosine, cosine], axis=1),
        jnp.concatenate([-sine, sine], axis=1),
    )


def start_pieces(piece_refs, groups, x_ref, sems):
    copies = []
    used = 0
    for k, group in enumerate(groups):
        start = k * OWNED
        here = []
        for rows in group:
            copy = pltpu.make_async_copy(
                piece_refs[used], x_ref.at[pl.ds(start, rows)], sems.at[used]
            )
            copy.start()
            here.append(copy)
            used += 1
            start += rows
        copies.append(here)
    return copies


def rope(u, cosine, sine):
    return u * cosine + pltpu.roll(u, HEAD // 2, 1) * sine


def place_of(z, k):
    return lax.rem(z - (0, 1, 3, 2)[k % 4] + 4, 4)


def table_rows(where, side):
    return pl.ds(pl.multiple_of(where * (2 * OWNED) + side * OWNED, OWNED), OWNED)


def project_kv_kernel(*refs, groups, other, tail):
    count = sum(len(group) for group in groups)
    place_ref = refs[0]
    wk_ref, wv_ref, cos_ref, sin_ref = refs[1 + count : 5 + count]
    kv_ref, x_ref, sems = refs[5 + count :]
    z = place_ref[0]
    side = 1 - place_ref[1] if other else place_ref[1]
    copies = start_pieces(refs[1 : 1 + count], groups, x_ref, sems)
    if tail:
        row = lax.broadcasted_iota(jnp.int32, (TAIL, 2 * HEAD), 0)
        ids = jnp.where(row < TAIL // 2, place_ref[2], place_ref[3])
        kv_ref[4 * OWNED :, :] = ids.astype(jnp.float32).astype(jnp.bfloat16)
    for half in range(2):
        for group in copies[2 * half : 2 * half + 2]:
            for copy in group:
                copy.wait()
        x = x_ref[half * 2 * OWNED : (half + 1) * 2 * OWNED, :]
        keys = jnp.dot(x, wk_ref[...], preferred_element_type=jnp.float32)
        values = jnp.dot(x, wv_ref[...], preferred_element_type=jnp.float32)
        for k in range(2):
            where = place_of(z, 2 * half + k)
            at = table_rows(where, side)
            mine = slice(k * OWNED, (k + 1) * OWNED)
            out = pl.ds(pl.multiple_of(where * OWNED, OWNED), OWNED)
            kv_ref[out, :HEAD] = rope(keys[mine], cos_ref[at, :], sin_ref[at, :]).astype(
                jnp.bfloat16
            )
            kv_ref[out, HEAD:] = values[mine].astype(jnp.bfloat16)


def project_q_kernel(*refs, groups):
    count = sum(len(group) for group in groups)
    place_ref = refs[0]
    wq_ref, cos_ref, sin_ref = refs[1 + count : 4 + count]
    q_ref, x_ref, sems = refs[4 + count :]
    z, side = place_ref[0], place_ref[1]
    copies = start_pieces(refs[1 : 1 + count], groups, x_ref, sems)
    for pair in range(len(groups) // 2):
        for group in copies[2 * pair : 2 * pair + 2]:
            for copy in group:
                copy.wait()
        x = x_ref[pair * 2 * OWNED : (pair + 1) * 2 * OWNED, :]
        query = jnp.dot(x, wq_ref[...], preferred_element_type=jnp.float32)
        for k in range(2):
            other = pair >= 2
            where = place_of(z, 2 * pair + k)
            at = table_rows(where, 1 - side if other else side)
            cosine, sine = cos_ref[at, :], sin_ref[at, :]
            mine = slice(k * OWNED, (k + 1) * OWNED)
            for h in range(query.shape[1] // HEAD):
                turned = rope(query[mine, h * HEAD : (h + 1) * HEAD], cosine, sine)
                turned = (turned * SCORE_SCALE).astype(jnp.bfloat16)
                for part in range(PARTS):
                    q_ref[int(other), part, where, h] = turned[
                        part * PIECE : (part + 1) * PIECE
                    ]


def project(kernel, place, groups, weights, tables, out):
    pieces = [piece for group in groups for piece in group]
    vmem = pl.BlockSpec(memory_space=pltpu.VMEM)
    smem = pl.BlockSpec(memory_space=pltpu.SMEM)
    hbm = pl.BlockSpec(memory_space=pl.ANY)
    width = weights[0].shape[0]
    columns = sum(w.shape[1] for w in weights)
    rows = len(groups) * OWNED
    return pl.pallas_call(
        functools.partial(
            kernel, groups=tuple(tuple(p.shape[0] for p in group) for group in groups)
        ),
        in_specs=[smem] + [hbm] * len(pieces) + [vmem] * (len(weights) + 2),
        out_specs=vmem,
        out_shape=jax.ShapeDtypeStruct(out, jnp.bfloat16),
        scratch_shapes=[
            pltpu.VMEM((rows, width), jnp.bfloat16),
            pltpu.SemaphoreType.DMA((len(pieces),)),
        ],
        compiler_params=pltpu.CompilerParams(vmem_limit_bytes=VMEM_LIMIT),
        cost_estimate=pl.CostEstimate(
            flops=2 * rows * width * columns,
            bytes_accessed=2 * width * (rows + columns),
            transcendentals=0,
        ),
    )(place, *pieces, *weights, *tables)


def attend_pairs(place_ref, off_ref, q_ref, kv_ref, state, tiles, per, heads, pairs, unroll, far):
    max_ref, sum_ref, acc_ref = state
    step = 2 * OWNED
    side = place_ref[1]

    def pair(which, block, masked):
        at = pl.multiple_of(off_ref[int(far), block], 16)
        keys = kv_ref[pl.ds(at, step), :HEAD]
        values = kv_ref[pl.ds(at, step), HEAD:]
        for start, part, other in tiles:
            here = pl.ds(pl.multiple_of(start + which * per, per), per)
            scores = lax.dot_general(
                q_ref[here, :], keys, (((1,), (1,)), ((), ())),
                preferred_element_type=jnp.float32,
            )
            if masked:
                row = lax.broadcasted_iota(jnp.int32, scores.shape, 0)
                row_side = 1 - side if other else side
                row = (
                    (row // (heads * PIECE)) * (2 * OWNED) + row_side * OWNED
                    + part * PIECE + (row & (PIECE - 1))
                )
                col = lax.broadcasted_iota(jnp.int32, scores.shape, 1)
                col_side = 1 - side if far else side
                col = (col // OWNED) * (2 * OWNED) + col_side * OWNED + (col & (OWNED - 1))
                scores = jnp.where(row >= col, scores, NEGATIVE)
            old = max_ref[here, :]
            new = jnp.maximum(old, jnp.max(scores, axis=1, keepdims=True))
            fade = jnp.exp2(old - new)
            weights = jnp.exp2(scores - jnp.concatenate([new] * (step // HEAD), axis=1))
            if masked:
                weights = jnp.where(row >= col, weights, 0.0)
            max_ref[here, :] = new
            added = weights[:, :HEAD]
            for u in range(1, step // HEAD):
                added = added + weights[:, u * HEAD : (u + 1) * HEAD]
            sum_ref[here, :] = sum_ref[here, :] * fade + added
            acc_ref[here, :] = acc_ref[here, :] * fade + jnp.dot(
                weights.astype(jnp.bfloat16), values, preferred_element_type=jnp.float32
            )

    first = place_ref[2]

    def plain(i):
        which = (i >= first).astype(jnp.int32)
        pair(which, i - which * first, False)

    def body(j, carry):
        for u in range(unroll):
            plain(j * unroll + u)
        return carry

    lax.fori_loop(0, pairs // unroll, body, 0)
    for i in range(pairs // unroll * unroll, pairs):
        plain(jnp.int32(i))
    for which in range(2):
        pair(which, place_ref[2 + which], True)


def attend_near_kernel(
    place_ref, off_ref, q_ref, kv_ref, max_ref, sum_ref, acc_ref, *, heads, pairs, unroll
):
    max_ref[...] = jnp.full_like(max_ref, NEGATIVE)
    sum_ref[...] = jnp.zeros_like(sum_ref)
    acc_ref[...] = jnp.zeros_like(acc_ref)
    per = 2 * heads * PIECE
    tiles = [
        ((other * PARTS + part) * 2 * per, part, bool(other))
        for other in range(2) for part in range(PARTS)
    ]
    attend_pairs(
        place_ref, off_ref, q_ref, kv_ref, (max_ref, sum_ref, acc_ref), tiles, per,
        heads, pairs, unroll, False,
    )


def attend_far_kernel(
    place_ref, off_ref, q_ref, kv_ref, max_in, sum_in, acc_in, o_ref,
    max_ref, sum_ref, acc_ref, *, part, other, heads, pairs, unroll,
):
    max_ref[...] = max_in[...]
    sum_ref[...] = sum_in[...]
    acc_ref[...] = acc_in[...]
    per = 2 * heads * PIECE
    attend_pairs(
        place_ref, off_ref, q_ref, kv_ref, (max_ref, sum_ref, acc_ref),
        [(0, part, other)], per, heads, pairs, unroll, True,
    )
    for group in range(4):
        for h in range(heads):
            start = (group * heads + h) * PIECE
            here = slice(start, start + PIECE)
            total = jnp.sum(sum_ref[here, :], axis=1, keepdims=True)
            o_ref[group * PIECE : (group + 1) * PIECE, h * HEAD : (h + 1) * HEAD] = (
                acc_ref[here, :] / total
            ).astype(jnp.bfloat16)


def attend_cost(pairs, rows, kv):
    scores = (pairs + 2) * rows * SPAN // 4
    return pl.CostEstimate(
        flops=scores * HEAD * 8, bytes_accessed=2 * kv.size + 12 * rows * HEAD,
        transcendentals=scores,
    )


def attend_near(place, offsets, query, kv, heads):
    pairs = offsets.shape[1] - 1
    vmem = pl.BlockSpec(memory_space=pltpu.VMEM)
    smem = pl.BlockSpec(memory_space=pltpu.SMEM)
    return pl.pallas_call(
        functools.partial(attend_near_kernel, heads=heads, pairs=pairs, unroll=6),
        in_specs=[smem, smem, vmem, vmem],
        out_specs=[vmem] * 3,
        out_shape=[jax.ShapeDtypeStruct(query.shape, jnp.float32)] * 3,
        compiler_params=pltpu.CompilerParams(vmem_limit_bytes=VMEM_LIMIT),
        cost_estimate=attend_cost(pairs, query.shape[0], kv),
    )(place, offsets, query, kv)


def attend_far(place, offsets, query, kv, state, part, other, heads):
    pairs = offsets.shape[1] - 1
    rows = 4 * heads * PIECE
    which = int(other) * PARTS + part
    chosen = pl.BlockSpec((rows, HEAD), lambda i: (which, 0))
    whole = pl.BlockSpec(kv.shape, lambda i: (0, 0))
    smem = pl.BlockSpec(memory_space=pltpu.SMEM)
    return pl.pallas_call(
        functools.partial(
            attend_far_kernel, part=part, other=other, heads=heads, pairs=pairs,
            unroll=10 if PARTS > 1 else 6,
        ),
        grid=(1,),
        in_specs=[smem, smem, chosen, whole] + [chosen] * 3,
        out_specs=pl.BlockSpec((4 * PIECE, heads * HEAD), lambda i: (0, 0)),
        out_shape=jax.ShapeDtypeStruct((4 * PIECE, heads * HEAD), jnp.bfloat16),
        scratch_shapes=[pltpu.VMEM((rows, HEAD), jnp.float32)] * 3,
        compiler_params=pltpu.CompilerParams(vmem_limit_bytes=VMEM_LIMIT),
        cost_estimate=attend_cost(pairs, rows, kv),
    )(place, offsets, query, kv, *state)


def combine_kernel(mine_ref, theirs_ref, w_mine_ref, w_theirs_ref, out_ref):
    out_ref[...] = (
        jnp.dot(mine_ref[...], w_mine_ref[...], preferred_element_type=jnp.float32)
        + jnp.dot(theirs_ref[...], w_theirs_ref[...], preferred_element_type=jnp.float32)
    ).astype(jnp.bfloat16)


def combine(mine, theirs, w_mine, w_theirs):
    rows, depth = mine.shape
    columns = w_mine.shape[1]
    step = 1024
    whole = lambda i: (0, 0)
    across = lambda i: (0, i)
    return pl.pallas_call(
        combine_kernel,
        grid=(columns // step,),
        in_specs=[
            pl.BlockSpec((rows, depth), whole),
            pl.BlockSpec((rows, depth), whole),
            pl.BlockSpec((depth, step), across),
            pl.BlockSpec((depth, step), across),
        ],
        out_specs=pl.BlockSpec((rows, step), across),
        out_shape=jax.ShapeDtypeStruct((rows, columns), jnp.bfloat16),
        compiler_params=pltpu.CompilerParams(vmem_limit_bytes=VMEM_LIMIT),
        cost_estimate=pl.CostEstimate(
            flops=4 * rows * depth * columns,
            bytes_accessed=4 * depth * columns + 2 * rows * columns,
            transcendentals=0,
        ),
    )(mine, theirs, w_mine, w_theirs)


def per_device(hidden_in, gain, positions, w_query, w_key, w_value, w_out, *, n_ctx):
    ids = positions[::SPAN] // SPAN
    place = jnp.concatenate(
        [jnp.stack([lax.axis_index("z"), lax.axis_index("y_hi")]).astype(jnp.int32), ids]
    )
    slices = 8
    part_rows = w_out.shape[0] // slices
    turn_of = lax.axis_index("x") * 2 + lax.axis_index("core")
    eighth = lax.dynamic_slice_in_dim(w_out, turn_of * part_rows, part_rows, 0)
    eighth = lax.ppermute(eighth, ("y_lo", "y_hi"), [(0, 3), (3, 0), (1, 2), (2, 1)])
    w_theirs = lax.all_gather(eighth, ("x", "core"), axis=0, tiled=True)

    widened = hidden_in.astype(jnp.float32)
    scale_rows = lax.rsqrt(jnp.mean(widened * widened, axis=-1, keepdims=True) + EPS)
    normed = (widened * scale_rows * gain.astype(jnp.float32)).astype(jnp.bfloat16)
    across = swap(normed)
    ahead, behind = turn(normed, 1), turn(normed, 3)
    late, across = lax.optimization_barrier((normed, across))
    near = [normed, ahead, behind, turn(late, 2)]
    crossed = [swap(ahead[DIRECT:]), swap(behind[DIRECT:])]
    tables = rope_tables(positions)
    *near, crossed[0], crossed[1], w_theirs = lax.optimization_barrier(
        (*near, *crossed, w_theirs)
    )
    kv_near = project(
        functools.partial(project_kv_kernel, other=False, tail=True),
        place, [[p] for p in near], (w_key, w_value), tables, (4 * OWNED + TAIL, 2 * HEAD),
    )
    kv_near_all = lax.all_gather(kv_near, CTX, axis=0, tiled=True)
    across, last, kv_near = lax.optimization_barrier((across, near[3], kv_near))
    far = [[across]] + [
        [turn(across[:DIRECT], by), piece]
        for by, piece in zip((1, 3, 2), (*crossed, swap(last[DIRECT:])))
    ]
    kv_far = project(
        functools.partial(project_kv_kernel, other=True, tail=False),
        place, far, (w_key, w_value), tables, (4 * OWNED, 2 * HEAD),
    )
    kv_near = kv_near_all
    kv_far_all = lax.all_gather(kv_far, CTX, axis=0, tiled=True)
    heads = w_query.shape[1] // HEAD
    query = project(
        project_q_kernel, place, [[p] for p in near] + far, (w_query,), tables,
        (2, PARTS, 4, heads, PIECE, HEAD),
    ).reshape(8 * heads * OWNED, HEAD)
    kv_far = kv_far_all

    rows_near = 4 * OWNED + TAIL
    known = kv_near.reshape(n_ctx, rows_near, 2 * HEAD)[:, 4 * OWNED :: TAIL // 2, 0]
    known = known.astype(jnp.int32).reshape(-1)
    owner = jnp.arange(2 * n_ctx, dtype=jnp.int32) // 2
    within = (jnp.arange(2 * n_ctx, dtype=jnp.int32) % 2) * (2 * OWNED)
    at = jnp.stack([owner * rows_near + within, owner * (4 * OWNED) + within])
    slots = jnp.arange(2 * n_ctx, dtype=jnp.int32)
    offsets = jnp.sum(
        jnp.where(known[None, :, None] == slots[None, None, :], at[:, :, None], 0), axis=1
    )

    state = attend_near(place, offsets, query, kv_near, heads)
    terms = []
    for part in range(PARTS):
        sent = attend_far(place, offsets, query, kv_far, state, part, True, heads)
        theirs = swap(sent)
        mine = attend_far(place, offsets, query, kv_far, state, part, False, heads)
        term = combine(mine, theirs, w_out, w_theirs)
        terms.append(lax.psum_scatter(term, "z", scatter_dimension=0, tiled=True))
    summed = jnp.concatenate(terms, axis=0).astype(jnp.float32)
    return (widened + summed).astype(jnp.bfloat16)


def solution(mesh):
    fine = Mesh(mesh.devices.reshape(2, 4, 2, 4, 2), AXES)
    rows = P(AXES, None)
    tp = AXES[3:]
    in_specs = (rows, P(), P(CTX), P(None, tp), P(None, tp), P(None, tp), P(tp, None))
    return jax.shard_map(
        functools.partial(per_device, n_ctx=mesh.shape["ctx"]),
        mesh=fine, in_specs=in_specs, out_specs=rows, check_vma=False,
    )
```

```python
import functools
import math

import jax
import jax.numpy as jnp
from jax import lax
from jax.experimental import pallas as pl
from jax.experimental.pallas import tpu as pltpu
from jax.sharding import Mesh
from jax.sharding import PartitionSpec as P

HEAD = 128
SPAN = 512
OWNED = 128
EPS = 1e-05
BASE = 500000.0
NEGATIVE = -1e30
HALF = OWNED // 2
DIRECT = (64, 96, 80)
TAIL = 16
VMEM_LIMIT = 56 * 2**20
SCORE_SCALE = math.log2(math.e) / HEAD**0.5

AXES = ("y_lo", "x", "core", "z", "y_hi")
CTX = AXES[:3]


def turn(x, by):
    return lax.ppermute(x, "z", [(i, (i + by) % 4) for i in range(4)])


def swap(x):
    return lax.ppermute(x, "y_hi", [(0, 1), (1, 0)])


def rope_tables(positions):
    half = HEAD // 2
    freq = BASE ** (-(jnp.arange(half, dtype=jnp.float32) * 2.0 / HEAD))
    angle = positions.astype(jnp.float32)[:, None] * freq[None, :]
    cosine, sine = jnp.cos(angle), jnp.sin(angle)
    return (
        jnp.concatenate([cosine, cosine], axis=1),
        jnp.concatenate([-sine, sine], axis=1),
    )


def start_pieces(piece_refs, groups, x_ref, sems):
    copies = []
    used = 0
    for k, group in enumerate(groups):
        start = k * OWNED
        here = []
        for rows in group:
            copy = pltpu.make_async_copy(
                piece_refs[used], x_ref.at[pl.ds(start, rows)], sems.at[used]
            )
            copy.start()
            here.append(copy)
            used += 1
            start += rows
        copies.append(here)
    return copies


def rope(u, cosine, sine):
    return u * cosine + pltpu.roll(u, HEAD // 2, 1) * sine


def place_of(z, k):
    return lax.rem(z - (0, 1, 3, 2)[k % 4] + 4, 4)


def table_rows(where, side):
    return pl.ds(pl.multiple_of(where * (2 * OWNED) + side * OWNED, OWNED), OWNED)


def project_kv_kernel(*refs, groups, other, tail):
    count = sum(len(group) for group in groups)
    place_ref = refs[0]
    w_ref, cos_ref, sin_ref = refs[1 + count : 4 + count]
    kv_ref, x_ref, sems = refs[4 + count :]
    z = place_ref[0]
    side = 1 - place_ref[1] if other else place_ref[1]
    copies = start_pieces(refs[1 : 1 + count], groups, x_ref, sems)
    if tail:
        row = lax.broadcasted_iota(jnp.int32, (TAIL, 2 * HEAD), 0)
        ids = jnp.where(row < TAIL // 2, place_ref[2], place_ref[3])
        kv_ref[4 * OWNED :, :] = ids.astype(jnp.float32).astype(jnp.bfloat16)
    for half in range(2):
        for group in copies[2 * half : 2 * half + 2]:
            for copy in group:
                copy.wait()
        x = x_ref[half * 2 * OWNED : (half + 1) * 2 * OWNED, :]
        both = jnp.dot(x, w_ref[...], preferred_element_type=jnp.float32)
        for k in range(2):
            where = place_of(z, 2 * half + k)
            at = table_rows(where, side)
            mine = slice(k * OWNED, (k + 1) * OWNED)
            out = pl.ds(pl.multiple_of(where * OWNED, OWNED), OWNED)
            kv_ref[out, :HEAD] = rope(both[mine, :HEAD], cos_ref[at, :], sin_ref[at, :]).astype(
                jnp.bfloat16
            )
            kv_ref[out, HEAD:] = both[mine, HEAD:].astype(jnp.bfloat16)


def project_q_kernel(*refs, groups, other):
    count = sum(len(group) for group in groups)
    place_ref = refs[0]
    wq_ref, cos_ref, sin_ref = refs[1 + count : 4 + count]
    q_ref, x_ref, sems = refs[4 + count :]
    z = place_ref[0]
    side = 1 - place_ref[1] if other else place_ref[1]
    copies = start_pieces(refs[1 : 1 + count], groups, x_ref, sems)
    for half in range(2):
        for group in copies[2 * half : 2 * half + 2]:
            for copy in group:
                copy.wait()
        x = x_ref[half * 2 * OWNED : (half + 1) * 2 * OWNED, :]
        query = jnp.dot(x, wq_ref[...], preferred_element_type=jnp.float32)
        for k in range(2):
            where = place_of(z, 2 * half + k)
            at = table_rows(where, side)
            cosine, sine = cos_ref[at, :], sin_ref[at, :]
            mine = slice(k * OWNED, (k + 1) * OWNED)
            for h in range(query.shape[1] // HEAD):
                turned = rope(query[mine, h * HEAD : (h + 1) * HEAD], cosine, sine)
                q_ref[where, h] = (turned * SCORE_SCALE).astype(jnp.bfloat16)


def project(kernel, place, groups, weights, tables, out):
    pieces = [piece for group in groups for piece in group]
    vmem = pl.BlockSpec(memory_space=pltpu.VMEM)
    smem = pl.BlockSpec(memory_space=pltpu.SMEM)
    hbm = pl.BlockSpec(memory_space=pl.ANY)
    width = weights[0].shape[0]
    columns = sum(w.shape[1] for w in weights)
    rows = len(groups) * OWNED
    return pl.pallas_call(
        functools.partial(
            kernel, groups=tuple(tuple(p.shape[0] for p in group) for group in groups)
        ),
        in_specs=[smem] + [hbm] * len(pieces) + [vmem] * (len(weights) + 2),
        out_specs=vmem,
        out_shape=jax.ShapeDtypeStruct(out, jnp.bfloat16),
        scratch_shapes=[
            pltpu.VMEM((rows, width), jnp.bfloat16),
            pltpu.SemaphoreType.DMA((len(pieces),)),
        ],
        compiler_params=pltpu.CompilerParams(vmem_limit_bytes=VMEM_LIMIT),
        cost_estimate=pl.CostEstimate(
            flops=2 * rows * width * columns,
            bytes_accessed=2 * width * (rows + columns),
            transcendentals=0,
        ),
    )(place, *pieces, *weights, *tables)


def attend_pairs(place_ref, off_ref, kv_ref, tiles, heads, pairs, unroll, far):
    per = 2 * heads * OWNED
    step = 2 * OWNED
    side = place_ref[1]

    def pair(which, block, masked):
        at = pl.multiple_of(off_ref[int(far), block], 16)
        keys = kv_ref[pl.ds(at, step), :HEAD]
        values = kv_ref[pl.ds(at, step), HEAD:]
        for other, q_ref, max_ref, sum_ref, acc_ref in tiles:
            here = pl.ds(pl.multiple_of(which * per, per), per)
            scores = lax.dot_general(
                q_ref[here, :], keys, (((1,), (1,)), ((), ())),
                preferred_element_type=jnp.float32,
            )
            if masked:
                row = lax.broadcasted_iota(jnp.int32, scores.shape, 0)
                row_side = 1 - side if other else side
                row = (
                    (row // (heads * OWNED)) * (2 * OWNED) + row_side * OWNED
                    + (row & (OWNED - 1))
                )
                col = lax.broadcasted_iota(jnp.int32, scores.shape, 1)
                col_side = 1 - side if far else side
                col = (col // OWNED) * (2 * OWNED) + col_side * OWNED + (col & (OWNED - 1))
                scores = jnp.where(row >= col, scores, NEGATIVE)
            old = max_ref[here, :]
            new = jnp.maximum(old, jnp.max(scores, axis=1, keepdims=True))
            fade = jnp.exp2(old - new)
            weights = jnp.exp2(scores - jnp.concatenate([new] * (step // HEAD), axis=1))
            if masked:
                weights = jnp.where(row >= col, weights, 0.0)
            max_ref[here, :] = new
            added = weights[:, :HEAD]
            for u in range(1, step // HEAD):
                added = added + weights[:, u * HEAD : (u + 1) * HEAD]
            sum_ref[here, :] = sum_ref[here, :] * fade + added
            acc_ref[here, :] = acc_ref[here, :] * fade + jnp.dot(
                weights.astype(jnp.bfloat16), values, preferred_element_type=jnp.float32
            )

    first = place_ref[2]

    def plain(i):
        which = (i >= first).astype(jnp.int32)
        pair(which, i - which * first, False)

    def body(j, carry):
        for u in range(unroll):
            plain(j * unroll + u)
        return carry

    lax.fori_loop(0, pairs // unroll, body, 0)
    for i in range(pairs // unroll * unroll, pairs):
        plain(jnp.int32(i))
    for which in range(2):
        pair(which, place_ref[2 + which], True)


def attend_near_kernel(
    place_ref, off_ref, q_near_ref, q_far_ref, kv_ref, *state_refs, heads, pairs, unroll
):
    for start in range(0, len(state_refs), 3):
        max_ref, sum_ref, acc_ref = state_refs[start : start + 3]
        max_ref[...] = jnp.full_like(max_ref, NEGATIVE)
        sum_ref[...] = jnp.zeros_like(sum_ref)
        acc_ref[...] = jnp.zeros_like(acc_ref)
    tiles = [(True, q_far_ref, *state_refs[3:]), (False, q_near_ref, *state_refs[:3])]
    attend_pairs(place_ref, off_ref, kv_ref, tiles, heads, pairs, unroll, False)


def attend_far_kernel(
    place_ref, off_ref, q_ref, kv_ref, max_in, sum_in, acc_in, o_ref,
    max_ref, sum_ref, acc_ref, *, other, heads, pairs, unroll,
):
    max_ref[...] = max_in[...]
    sum_ref[...] = sum_in[...]
    acc_ref[...] = acc_in[...]
    tiles = [(other, q_ref, max_ref, sum_ref, acc_ref)]
    attend_pairs(place_ref, off_ref, kv_ref, tiles, heads, pairs, unroll, True)
    for group in range(4):
        for h in range(heads):
            start = (group * heads + h) * OWNED
            here = slice(start, start + OWNED)
            total = jnp.sum(sum_ref[here, :], axis=1, keepdims=True)
            o_ref[group * OWNED : (group + 1) * OWNED, h * HEAD : (h + 1) * HEAD] = (
                acc_ref[here, :] / total
            ).astype(jnp.bfloat16)


def attend_cost(pairs, rows, kv):
    scores = (pairs + 2) * rows * SPAN // 4
    return pl.CostEstimate(
        flops=scores * HEAD * 8, bytes_accessed=2 * kv.size + 12 * rows * HEAD,
        transcendentals=scores,
    )


def attend_near(place, offsets, q_near, q_far, kv, heads):
    pairs = offsets.shape[1] - 1
    vmem = pl.BlockSpec(memory_space=pltpu.VMEM)
    smem = pl.BlockSpec(memory_space=pltpu.SMEM)
    return pl.pallas_call(
        functools.partial(attend_near_kernel, heads=heads, pairs=pairs, unroll=6),
        in_specs=[smem, smem, vmem, vmem, vmem],
        out_specs=[vmem] * 6,
        out_shape=[jax.ShapeDtypeStruct(q_near.shape, jnp.float32)] * 6,
        compiler_params=pltpu.CompilerParams(vmem_limit_bytes=VMEM_LIMIT),
        cost_estimate=attend_cost(pairs, 2 * q_near.shape[0], kv),
    )(place, offsets, q_near, q_far, kv)


def attend_far(place, offsets, query, kv, state, other, heads):
    pairs = offsets.shape[1] - 1
    vmem = pl.BlockSpec(memory_space=pltpu.VMEM)
    smem = pl.BlockSpec(memory_space=pltpu.SMEM)
    return pl.pallas_call(
        functools.partial(
            attend_far_kernel, other=other, heads=heads, pairs=pairs, unroll=10
        ),
        in_specs=[smem, smem] + [vmem] * 5,
        out_specs=vmem,
        out_shape=jax.ShapeDtypeStruct((4 * OWNED, heads * HEAD), jnp.bfloat16),
        scratch_shapes=[pltpu.VMEM(query.shape, jnp.float32)] * 3,
        compiler_params=pltpu.CompilerParams(vmem_limit_bytes=VMEM_LIMIT),
        cost_estimate=attend_cost(pairs, query.shape[0], kv),
    )(place, offsets, query, kv, *state)


def combine_kernel(mine_ref, theirs_ref, w_mine_ref, w_theirs_ref, out_ref):
    out_ref[...] = (
        jnp.dot(mine_ref[...], w_mine_ref[...], preferred_element_type=jnp.float32)
        + jnp.dot(theirs_ref[...], w_theirs_ref[...], preferred_element_type=jnp.float32)
    ).astype(jnp.bfloat16)


def combine(mine, theirs, w_mine, w_theirs):
    rows, depth = mine.shape
    columns = w_mine.shape[1]
    step = 512
    whole = lambda i: (0, 0)
    across = lambda i: (0, i)
    return pl.pallas_call(
        combine_kernel,
        grid=(columns // step,),
        in_specs=[
            pl.BlockSpec((rows, depth), whole),
            pl.BlockSpec((rows, depth), whole),
            pl.BlockSpec((depth, step), across),
            pl.BlockSpec((depth, step), across),
        ],
        out_specs=pl.BlockSpec((rows, step), lambda i: (0, i)),
        out_shape=jax.ShapeDtypeStruct((rows, columns), jnp.bfloat16),
        compiler_params=pltpu.CompilerParams(vmem_limit_bytes=VMEM_LIMIT),
        cost_estimate=pl.CostEstimate(
            flops=4 * rows * depth * columns,
            bytes_accessed=4 * depth * columns + 2 * rows * columns,
            transcendentals=0,
        ),
    )(mine, theirs, w_mine, w_theirs)


def per_device(hidden_in, gain, positions, w_query, w_key, w_value, w_out, *, n_ctx):
    ids = positions[::SPAN] // SPAN
    place = jnp.concatenate(
        [jnp.stack([lax.axis_index("z"), lax.axis_index("y_hi")]).astype(jnp.int32), ids]
    )
    widened = hidden_in.astype(jnp.float32)
    scale_rows = lax.rsqrt(jnp.mean(widened * widened, axis=-1, keepdims=True) + EPS)
    normed = (widened * scale_rows * gain.astype(jnp.float32)).astype(jnp.bfloat16)
    across, ahead, behind = lax.optimization_barrier(
        (swap(normed), turn(normed, 1), turn(normed, 3))
    )
    opposite = [turn(ahead[:HALF], 1), turn(behind[HALF:], 3)]
    near = [[normed], [ahead], [behind], opposite]
    crossed = swap(ahead[DIRECT[0] :])
    tables = rope_tables(positions)
    w_kv = jnp.concatenate([w_key, w_value], axis=1)
    near, crossed, w_kv = lax.optimization_barrier((near, crossed, w_kv))
    kv_near = project(
        functools.partial(project_kv_kernel, other=False, tail=True),
        place, near, (w_kv,), tables, (4 * OWNED + TAIL, 2 * HEAD),
    )
    kv_near_all = lax.all_gather(kv_near, CTX, axis=0, tiled=True)
    across, near, kv_near = lax.optimization_barrier((across, near, kv_near))
    far = [
        [across],
        [turn(across[: DIRECT[0]], 1), crossed],
        [turn(across[: DIRECT[1]], 3), swap(near[2][0][DIRECT[1] :])],
        [turn(across[: DIRECT[2]], 2), swap(near[3][1][DIRECT[2] - HALF :])],
    ]
    heads = w_query.shape[1] // HEAD

    def queries(groups, other):
        return project(
            functools.partial(project_q_kernel, other=other),
            place, groups, (w_query,), tables, (4, heads, OWNED, HEAD),
        ).reshape(4 * heads * OWNED, HEAD)

    q_near = queries(near, False)
    far, q_near = lax.optimization_barrier((far, q_near))
    kv_far = project(
        functools.partial(project_kv_kernel, other=True, tail=False),
        place, far, (w_kv,), tables, (4 * OWNED, 2 * HEAD),
    )
    kv_near = kv_near_all
    kv_far_all = lax.all_gather(kv_far, CTX, axis=0, tiled=True)
    q_far = queries(far, True)
    slices = 8
    part_rows = w_out.shape[0] // slices
    turn_of = lax.axis_index("x") * 2 + lax.axis_index("core")
    eighth = lax.dynamic_slice_in_dim(w_out, turn_of * part_rows, part_rows, 0)
    eighth, _ = lax.optimization_barrier((eighth, kv_far))
    eighth = lax.ppermute(eighth, ("y_lo", "y_hi"), [(0, 3), (3, 0), (1, 2), (2, 1)])
    eighth, q_far = lax.optimization_barrier((eighth, q_far))
    kv_far = kv_far_all
    w_theirs = lax.all_gather(eighth, ("x", "core"), axis=0, tiled=True)

    rows_near = 4 * OWNED + TAIL
    known = kv_near.reshape(n_ctx, rows_near, 2 * HEAD)[:, 4 * OWNED :: TAIL // 2, 0]
    known = known.astype(jnp.int32).reshape(-1)
    owner = jnp.arange(2 * n_ctx, dtype=jnp.int32) // 2
    within = (jnp.arange(2 * n_ctx, dtype=jnp.int32) % 2) * (2 * OWNED)
    at = jnp.stack([owner * rows_near + within, owner * (4 * OWNED) + within])
    slots = jnp.arange(2 * n_ctx, dtype=jnp.int32)
    offsets = jnp.sum(
        jnp.where(known[None, :, None] == slots[None, None, :], at[:, :, None], 0), axis=1
    )

    state = attend_near(place, offsets, q_near, q_far, kv_near, heads)
    sent = attend_far(place, offsets, q_far, kv_far, state[3:], True, heads)
    theirs = swap(sent)
    mine = attend_far(place, offsets, q_near, kv_far, state[:3], False, heads)
    term = combine(mine, theirs, w_out, w_theirs)
    summed = lax.psum_scatter(term, "z", scatter_dimension=0, tiled=True)
    return (widened + summed.astype(jnp.float32)).astype(jnp.bfloat16)


def solution(mesh):
    fine = Mesh(mesh.devices.reshape(2, 4, 2, 4, 2), AXES)
    rows = P(AXES, None)
    tp = AXES[3:]
    in_specs = (rows, P(), P(CTX), P(None, tp), P(None, tp), P(None, tp), P(tp, None))
    return jax.shard_map(
        functools.partial(per_device, n_ctx=mesh.shape["ctx"]),
        mesh=fine, in_specs=in_specs, out_specs=rows, check_vma=False,
    )
```

```python
import functools
import math

import jax
import jax.numpy as jnp
from jax import lax
from jax.experimental import pallas as pl
from jax.experimental.pallas import tpu as pltpu
from jax.sharding import Mesh
from jax.sharding import PartitionSpec as P

HEAD = 128
SPAN = 512
OWNED = 128
EPS = 1e-05
BASE = 500000.0
NEGATIVE = -1e30
HALF = OWNED // 2
PARTS = 1
PIECE = OWNED // PARTS
DIRECT = (64, 96, 80)
TAIL = 16
VMEM_LIMIT = 56 * 2**20
SCORE_SCALE = math.log2(math.e) / HEAD**0.5

AXES = ("y_lo", "x", "core", "z", "y_hi")
CTX = AXES[:3]


def turn(x, by):
    return lax.ppermute(x, "z", [(i, (i + by) % 4) for i in range(4)])


def swap(x):
    return lax.ppermute(x, "y_hi", [(0, 1), (1, 0)])


def rope_tables(positions):
    half = HEAD // 2
    freq = BASE ** (-(jnp.arange(half, dtype=jnp.float32) * 2.0 / HEAD))
    angle = positions.astype(jnp.float32)[:, None] * freq[None, :]
    cosine, sine = jnp.cos(angle), jnp.sin(angle)
    return (
        jnp.concatenate([cosine, cosine], axis=1),
        jnp.concatenate([-sine, sine], axis=1),
    )


def start_pieces(piece_refs, groups, x_ref, sems):
    copies = []
    used = 0
    for k, group in enumerate(groups):
        start = k * OWNED
        here = []
        for rows in group:
            copy = pltpu.make_async_copy(
                piece_refs[used], x_ref.at[pl.ds(start, rows)], sems.at[used]
            )
            copy.start()
            here.append(copy)
            used += 1
            start += rows
        copies.append(here)
    return copies


def rope(u, cosine, sine):
    return u * cosine + pltpu.roll(u, HEAD // 2, 1) * sine


def place_of(z, k):
    return lax.rem(z - (0, 1, 3, 2)[k % 4] + 4, 4)


def table_rows(where, side):
    return pl.ds(pl.multiple_of(where * (2 * OWNED) + side * OWNED, OWNED), OWNED)


def project_kv_kernel(*refs, groups, other, tail):
    count = sum(len(group) for group in groups)
    place_ref = refs[0]
    w_ref, cos_ref, sin_ref = refs[1 + count : 4 + count]
    kv_ref, x_ref, sems = refs[4 + count :]
    z = place_ref[0]
    side = 1 - place_ref[1] if other else place_ref[1]
    copies = start_pieces(refs[1 : 1 + count], groups, x_ref, sems)
    if tail:
        row = lax.broadcasted_iota(jnp.int32, (TAIL, 2 * HEAD), 0)
        ids = jnp.where(row < TAIL // 2, place_ref[2], place_ref[3])
        kv_ref[4 * OWNED :, :] = ids.astype(jnp.float32).astype(jnp.bfloat16)
    for half in range(2):
        for group in copies[2 * half : 2 * half + 2]:
            for copy in group:
                copy.wait()
        x = x_ref[half * 2 * OWNED : (half + 1) * 2 * OWNED, :]
        both = jnp.dot(x, w_ref[...], preferred_element_type=jnp.float32)
        for k in range(2):
            where = place_of(z, 2 * half + k)
            at = table_rows(where, side)
            mine = slice(k * OWNED, (k + 1) * OWNED)
            out = pl.ds(pl.multiple_of(where * OWNED, OWNED), OWNED)
            kv_ref[out, :HEAD] = rope(both[mine, :HEAD], cos_ref[at, :], sin_ref[at, :]).astype(
                jnp.bfloat16
            )
            kv_ref[out, HEAD:] = both[mine, HEAD:].astype(jnp.bfloat16)


def project_q_kernel(*refs, groups, other):
    count = sum(len(group) for group in groups)
    place_ref = refs[0]
    wq_ref, cos_ref, sin_ref = refs[1 + count : 4 + count]
    q_ref, x_ref, sems = refs[4 + count :]
    z = place_ref[0]
    side = 1 - place_ref[1] if other else place_ref[1]
    copies = start_pieces(refs[1 : 1 + count], groups, x_ref, sems)
    for half in range(2):
        for group in copies[2 * half : 2 * half + 2]:
            for copy in group:
                copy.wait()
        x = x_ref[half * 2 * OWNED : (half + 1) * 2 * OWNED, :]
        query = jnp.dot(x, wq_ref[...], preferred_element_type=jnp.float32)
        for k in range(2):
            where = place_of(z, 2 * half + k)
            at = table_rows(where, side)
            cosine, sine = cos_ref[at, :], sin_ref[at, :]
            mine = slice(k * OWNED, (k + 1) * OWNED)
            for h in range(query.shape[1] // HEAD):
                turned = rope(query[mine, h * HEAD : (h + 1) * HEAD], cosine, sine)
                turned = (turned * SCORE_SCALE).astype(jnp.bfloat16)
                for part in range(PARTS):
                    q_ref[part, where, h] = turned[part * PIECE : (part + 1) * PIECE]


def project(kernel, place, groups, weights, tables, out):
    pieces = [piece for group in groups for piece in group]
    vmem = pl.BlockSpec(memory_space=pltpu.VMEM)
    smem = pl.BlockSpec(memory_space=pltpu.SMEM)
    hbm = pl.BlockSpec(memory_space=pl.ANY)
    width = weights[0].shape[0]
    columns = sum(w.shape[1] for w in weights)
    rows = len(groups) * OWNED
    return pl.pallas_call(
        functools.partial(
            kernel, groups=tuple(tuple(p.shape[0] for p in group) for group in groups)
        ),
        in_specs=[smem] + [hbm] * len(pieces) + [vmem] * (len(weights) + 2),
        out_specs=vmem,
        out_shape=jax.ShapeDtypeStruct(out, jnp.bfloat16),
        scratch_shapes=[
            pltpu.VMEM((rows, width), jnp.bfloat16),
            pltpu.SemaphoreType.DMA((len(pieces),)),
        ],
        compiler_params=pltpu.CompilerParams(vmem_limit_bytes=VMEM_LIMIT),
        cost_estimate=pl.CostEstimate(
            flops=2 * rows * width * columns,
            bytes_accessed=2 * width * (rows + columns),
            transcendentals=0,
        ),
    )(place, *pieces, *weights, *tables)


def start_keys(place_ref, kv_ref, held_ref, sems, n_ctx):
    stride = kv_ref.shape[0] // n_ctx
    copies = []
    for t in range(n_ctx):
        at = pl.multiple_of(lax.rem(place_ref[4] + 1 + t, n_ctx) * stride, 16)
        rows = pl.ds(at, stride)
        copy = pltpu.make_async_copy(kv_ref.at[rows], held_ref.at[rows], sems.at[t])
        copy.start()
        copies.append(copy)
    return copies


def attend_pairs(place_ref, known_ref, kv_ref, held_ref, sems, tiles, heads, far):
    per = 2 * heads * PIECE
    step = 2 * OWNED
    side = place_ref[1]
    n_ctx = sems.shape[0]
    stride = kv_ref.shape[0] // n_ctx
    me = place_ref[4]
    early = (place_ref[2] > place_ref[3]).astype(jnp.int32)
    earliest = jnp.minimum(place_ref[2], place_ref[3])

    def peer(i):
        one, two = known_ref[2 * i], known_ref[2 * i + 1]
        return (one > two).astype(jnp.int32), jnp.minimum(one, two)

    def pair(which, i, half, masked):
        at = pl.multiple_of(i * stride + half * step, 16)
        keys = held_ref[pl.ds(at, step), :HEAD]
        values = held_ref[pl.ds(at, step), HEAD:]
        for other, part, q_ref, max_ref, sum_ref, acc_ref in tiles:
            here = pl.ds(pl.multiple_of(which * per, per), per)
            scores = lax.dot_general(
                q_ref[here, :], keys, (((1,), (1,)), ((), ())),
                preferred_element_type=jnp.float32,
            )
            if masked:
                row = lax.broadcasted_iota(jnp.int32, scores.shape, 0)
                row_side = 1 - side if other else side
                row = (
                    (row // (heads * PIECE)) * (2 * OWNED) + row_side * OWNED
                    + part * PIECE + (row & (PIECE - 1))
                )
                col = lax.broadcasted_iota(jnp.int32, scores.shape, 1)
                col_side = 1 - side if far else side
                col = (col // OWNED) * (2 * OWNED) + col_side * OWNED + (col & (OWNED - 1))
                scores = jnp.where(row >= col, scores, NEGATIVE)
            old = max_ref[here, :]
            new = jnp.maximum(old, jnp.max(scores, axis=1, keepdims=True))
            fade = jnp.exp2(old - new)
            weights = jnp.exp2(scores - jnp.concatenate([new] * (step // HEAD), axis=1))
            if masked:
                weights = jnp.where(row >= col, weights, 0.0)
            max_ref[here, :] = new
            added = weights[:, :HEAD]
            for u in range(1, step // HEAD):
                added = added + weights[:, u * HEAD : (u + 1) * HEAD]
            sum_ref[here, :] = sum_ref[here, :] * fade + added
            acc_ref[here, :] = acc_ref[here, :] * fade + jnp.dot(
                weights.astype(jnp.bfloat16), values, preferred_element_type=jnp.float32
            )

    group = 5 if (n_ctx - 1) % 5 == 0 else 1

    def wait(t):
        rows = pl.ds(0, stride)
        pltpu.make_async_copy(kv_ref.at[rows], held_ref.at[rows], sems.at[t]).wait()

    def body(j, carry):
        for u in range(group):
            wait(j * group + u)
        for u in range(group):
            i = lax.rem(me + 1 + j * group + u, n_ctx)
            lower, least = peer(i)
            pair(1 - early, i, lower, False)
            before = (least < earliest).astype(jnp.int32)
            pair(
                before * early + (1 - before) * (1 - early),
                i, before * lower + (1 - before) * (1 - lower), False,
            )
        return carry

    lax.fori_loop(0, (n_ctx - 1) // group, body, 0)
    wait(n_ctx - 1)
    pair(1 - early, me, early, False)
    for which in range(2):
        pair(which, me, which, True)


def attend_near_kernel(
    place_ref, known_ref, q_near_ref, q_far_ref, kv_ref, *refs, heads, n_ctx
):
    state_refs, (held_ref, sems) = refs[:-2], refs[-2:]
    start_keys(place_ref, kv_ref, held_ref, sems, n_ctx)
    tiles = []
    for index in range(2 * PARTS):
        max_ref, sum_ref, acc_ref = state_refs[3 * index : 3 * index + 3]
        max_ref[...] = jnp.full_like(max_ref, NEGATIVE)
        sum_ref[...] = jnp.zeros_like(sum_ref)
        acc_ref[...] = jnp.zeros_like(acc_ref)
        other, part = index >= PARTS, index % PARTS
        q_ref = (q_far_ref if other else q_near_ref).at[part]
        tiles.append((other, part, q_ref, max_ref, sum_ref, acc_ref))
    attend_pairs(place_ref, known_ref, kv_ref, held_ref, sems, tiles, heads, False)


def attend_far_kernel(
    place_ref, known_ref, q_ref, kv_ref, max_in, sum_in, acc_in, o_ref,
    max_ref, sum_ref, acc_ref, held_ref, sems, *, other, part, heads, n_ctx,
):
    start_keys(place_ref, kv_ref, held_ref, sems, n_ctx)
    max_ref[...] = max_in[...]
    sum_ref[...] = sum_in[...]
    acc_ref[...] = acc_in[...]
    tiles = [(other, part, q_ref, max_ref, sum_ref, acc_ref)]
    attend_pairs(place_ref, known_ref, kv_ref, held_ref, sems, tiles, heads, True)
    for group in range(4):
        for h in range(heads):
            start = (group * heads + h) * PIECE
            here = slice(start, start + PIECE)
            total = jnp.sum(sum_ref[here, :], axis=1, keepdims=True)
            o_ref[group * PIECE : (group + 1) * PIECE, h * HEAD : (h + 1) * HEAD] = (
                acc_ref[here, :] / total
            ).astype(jnp.bfloat16)


def attend_cost(n_ctx, rows, kv):
    scores = (2 * n_ctx + 1) * rows * SPAN // 4
    return pl.CostEstimate(
        flops=scores * HEAD * 8, bytes_accessed=2 * kv.size + 12 * rows * HEAD,
        transcendentals=scores,
    )


def attend_near(place, known, q_near, q_far, kv, heads):
    n_ctx = known.shape[0] // 2
    vmem = pl.BlockSpec(memory_space=pltpu.VMEM)
    smem = pl.BlockSpec(memory_space=pltpu.SMEM)
    return pl.pallas_call(
        functools.partial(attend_near_kernel, heads=heads, n_ctx=n_ctx),
        in_specs=[smem, smem, vmem, vmem, pl.BlockSpec(memory_space=pl.ANY)],
        out_specs=[vmem] * (6 * PARTS),
        out_shape=[jax.ShapeDtypeStruct(q_near.shape[1:], jnp.float32)] * (6 * PARTS),
        scratch_shapes=[
            pltpu.VMEM(kv.shape, jnp.bfloat16), pltpu.SemaphoreType.DMA((n_ctx,)),
        ],
        compiler_params=pltpu.CompilerParams(vmem_limit_bytes=VMEM_LIMIT),
        cost_estimate=attend_cost(n_ctx, 2 * PARTS * q_near.shape[1], kv),
    )(place, known, q_near, q_far, kv)


def attend_far(place, known, query, kv, state, other, part, heads):
    n_ctx = known.shape[0] // 2
    vmem = pl.BlockSpec(memory_space=pltpu.VMEM)
    smem = pl.BlockSpec(memory_space=pltpu.SMEM)
    return pl.pallas_call(
        functools.partial(
            attend_far_kernel, other=other, part=part, heads=heads, n_ctx=n_ctx
        ),
        in_specs=[smem, smem, vmem, pl.BlockSpec(memory_space=pl.ANY)] + [vmem] * 3,
        out_specs=vmem,
        out_shape=jax.ShapeDtypeStruct((4 * PIECE, heads * HEAD), jnp.bfloat16),
        scratch_shapes=[pltpu.VMEM(query.shape, jnp.float32)] * 3 + [
            pltpu.VMEM(kv.shape, jnp.bfloat16), pltpu.SemaphoreType.DMA((n_ctx,)),
        ],
        compiler_params=pltpu.CompilerParams(vmem_limit_bytes=VMEM_LIMIT),
        cost_estimate=attend_cost(n_ctx, query.shape[0], kv),
    )(place, known, query, kv, *state)


def combine_kernel(core_ref, mine_ref, theirs_ref, w_mine_ref, w_own_ref, w_other_ref, out_ref):
    half = theirs_ref.shape[1] // 2
    theirs = theirs_ref[...]
    low = core_ref[0] == 0
    own = jnp.where(low, theirs[:, :half], theirs[:, half:])
    other = jnp.where(low, theirs[:, half:], theirs[:, :half])
    out_ref[...] = (
        jnp.dot(mine_ref[...], w_mine_ref[...], preferred_element_type=jnp.float32)
        + jnp.dot(own, w_own_ref[...], preferred_element_type=jnp.float32)
        + jnp.dot(other, w_other_ref[...], preferred_element_type=jnp.float32)
    ).astype(jnp.bfloat16)


def combine(core, mine, theirs, w_mine, w_own, w_other):
    rows, depth = mine.shape
    columns = w_mine.shape[1]
    step = 1024
    whole = lambda i: (0, 0)
    across = lambda i: (0, i)
    return pl.pallas_call(
        combine_kernel,
        grid=(columns // step,),
        in_specs=[
            pl.BlockSpec(memory_space=pltpu.SMEM),
            pl.BlockSpec((rows, depth), whole),
            pl.BlockSpec((rows, depth), whole),
            pl.BlockSpec((depth, step), across),
            pl.BlockSpec((depth // 2, step), across),
            pl.BlockSpec((depth // 2, step), across),
        ],
        out_specs=pl.BlockSpec((rows, step), across),
        out_shape=jax.ShapeDtypeStruct((rows, columns), jnp.bfloat16),
        compiler_params=pltpu.CompilerParams(vmem_limit_bytes=14 * 2**20),
        cost_estimate=pl.CostEstimate(
            flops=4 * rows * depth * columns,
            bytes_accessed=4 * depth * columns + 2 * rows * columns,
            transcendentals=0,
        ),
    )(core, mine, theirs, w_mine, w_own, w_other)


def per_device(hidden_in, gain, positions, w_query, w_key, w_value, w_out, *, n_ctx):
    ids = positions[::SPAN] // SPAN
    place = jnp.concatenate(
        [
            jnp.stack([lax.axis_index("z"), lax.axis_index("y_hi")]).astype(jnp.int32), ids,
            lax.axis_index(CTX).astype(jnp.int32).reshape(1),
        ]
    )
    widened = hidden_in.astype(jnp.float32)
    scale_rows = lax.rsqrt(jnp.mean(widened * widened, axis=-1, keepdims=True) + EPS)
    normed = (widened * scale_rows * gain.astype(jnp.float32)).astype(jnp.bfloat16)
    across, ahead, behind = lax.optimization_barrier(
        (swap(normed), turn(normed, 1), turn(normed, 3))
    )
    opposite = [turn(ahead[:HALF], 1), turn(behind[HALF:], 3)]
    near = [[normed], [ahead], [behind], opposite]
    crossed = swap(ahead[DIRECT[0] :])
    tables = rope_tables(positions)
    w_kv = jnp.concatenate([w_key, w_value], axis=1)
    near, crossed, w_kv = lax.optimization_barrier((near, crossed, w_kv))
    kv_near = project(
        functools.partial(project_kv_kernel, other=False, tail=True),
        place, near, (w_kv,), tables, (4 * OWNED + TAIL, 2 * HEAD),
    )
    kv_near_all = lax.all_gather(kv_near, CTX, axis=0, tiled=True)
    across, near, kv_near = lax.optimization_barrier((across, near, kv_near))
    far = [
        [across],
        [turn(across[: DIRECT[0]], 1), crossed],
        [turn(across[: DIRECT[1]], 3), swap(near[2][0][DIRECT[1] :])],
        [turn(across[: DIRECT[2]], 2), swap(near[3][1][DIRECT[2] - HALF :])],
    ]
    heads = w_query.shape[1] // HEAD

    def queries(groups, other):
        return project(
            functools.partial(project_q_kernel, other=other),
            place, groups, (w_query,), tables, (PARTS, 4, heads, PIECE, HEAD),
        ).reshape(PARTS, 4 * heads * PIECE, HEAD)

    q_near = queries(near, False)
    far, q_near = lax.optimization_barrier((far, q_near))
    kv_far = project(
        functools.partial(project_kv_kernel, other=True, tail=False),
        place, far, (w_kv,), tables, (4 * OWNED, 2 * HEAD),
    )
    kv_near = kv_near_all
    kv_far_all = lax.all_gather(kv_far, CTX, axis=0, tiled=True)
    q_far = queries(far, True)
    kv_far, q_far = lax.optimization_barrier((kv_far, q_far))
    core = lax.axis_index("core").astype(jnp.int32)
    half_rows = w_out.shape[0] // 2
    w_own = lax.dynamic_slice_in_dim(w_out, core * half_rows, half_rows, 0)
    w_own, _ = lax.optimization_barrier((w_own, far))
    w_own = lax.ppermute(w_own, ("y_lo", "y_hi"), [(0, 3), (3, 0), (1, 2), (2, 1)])
    kv_far = kv_far_all
    rows_near = 4 * OWNED + TAIL
    known = kv_near.reshape(n_ctx, rows_near, 2 * HEAD)[:, 4 * OWNED :: TAIL // 2, 0]
    known = known.astype(jnp.int32).reshape(-1)
    state = attend_near(place, known, q_near, q_far, kv_near, heads)
    terms = []
    for part in range(PARTS):
        mine, sent = state[3 * part : 3 * part + 3], state[3 * (PARTS + part) :][:3]
        sent = attend_far(place, known, q_far[part], kv_far, sent, True, part, heads)
        if part == 0:
            sent, w_own = lax.optimization_barrier((sent, w_own))
            w_other = lax.ppermute(w_own, "core", [(0, 1), (1, 0)])
        theirs = swap(sent)
        mine = attend_far(place, known, q_near[part], kv_far, mine, False, part, heads)
        term = combine(core.reshape(1), mine, theirs, w_out, w_own, w_other)
        terms.append(lax.psum_scatter(term, "z", scatter_dimension=0, tiled=True))
    summed = jnp.concatenate(terms, axis=0).astype(jnp.float32)
    return (widened + summed).astype(jnp.bfloat16)


def solution(mesh):
    fine = Mesh(mesh.devices.reshape(2, 4, 2, 4, 2), AXES)
    rows = P(AXES, None)
    tp = AXES[3:]
    in_specs = (rows, P(), P(CTX), P(None, tp), P(None, tp), P(None, tp), P(tp, None))
    return jax.shard_map(
        functools.partial(per_device, n_ctx=mesh.shape["ctx"]),
        mesh=fine, in_specs=in_specs, out_specs=rows, check_vma=False,
    )
```

```python
import functools
import math

import jax
import jax.numpy as jnp
from jax import lax
from jax.experimental import pallas as pl
from jax.experimental.pallas import tpu as pltpu
from jax.sharding import Mesh
from jax.sharding import PartitionSpec as P

HEAD = 128
SPAN = 512
OWNED = 128
EPS = 1e-05
BASE = 500000.0
NEGATIVE = -1e30
HALF = OWNED // 2
PARTS = 1
PIECE = OWNED // PARTS
DIRECT = (64, 96, 80)
TAIL = 16
VMEM_LIMIT = 56 * 2**20
SCORE_SCALE = math.log2(math.e) / HEAD**0.5

AXES = ("y_lo", "x", "core", "z", "y_hi")
CTX = AXES[:3]


def turn(x, by):
    return lax.ppermute(x, "z", [(i, (i + by) % 4) for i in range(4)])


def swap(x):
    return lax.ppermute(x, "y_hi", [(0, 1), (1, 0)])


def rope_tables(positions):
    half = HEAD // 2
    freq = BASE ** (-(jnp.arange(half, dtype=jnp.float32) * 2.0 / HEAD))
    angle = positions.astype(jnp.float32)[:, None] * freq[None, :]
    cosine, sine = jnp.cos(angle), jnp.sin(angle)
    return (
        jnp.concatenate([cosine, cosine], axis=1),
        jnp.concatenate([-sine, sine], axis=1),
    )


def start_pieces(piece_refs, groups, x_ref, sems):
    copies = []
    used = 0
    for k, group in enumerate(groups):
        start = k * OWNED
        here = []
        for rows in group:
            copy = pltpu.make_async_copy(
                piece_refs[used], x_ref.at[pl.ds(start, rows)], sems.at[used]
            )
            copy.start()
            here.append(copy)
            used += 1
            start += rows
        copies.append(here)
    return copies


def rope(u, cosine, sine):
    return u * cosine + pltpu.roll(u, HEAD // 2, 1) * sine


def place_of(z, k):
    return lax.rem(z - (0, 1, 3, 2)[k % 4] + 4, 4)


def table_rows(where, side):
    return pl.ds(pl.multiple_of(where * (2 * OWNED) + side * OWNED, OWNED), OWNED)


def project_kv_kernel(*refs, groups, other, tail):
    count = sum(len(group) for group in groups)
    place_ref = refs[0]
    w_ref, cos_ref, sin_ref = refs[1 + count : 4 + count]
    kv_ref, x_ref, sems = refs[4 + count :]
    z = place_ref[0]
    side = 1 - place_ref[1] if other else place_ref[1]
    copies = start_pieces(refs[1 : 1 + count], groups, x_ref, sems)
    if tail:
        row = lax.broadcasted_iota(jnp.int32, (TAIL, 2 * HEAD), 0)
        ids = jnp.where(row < TAIL // 2, place_ref[2], place_ref[3])
        kv_ref[4 * OWNED :, :] = ids.astype(jnp.float32).astype(jnp.bfloat16)
    for half in range(2):
        for group in copies[2 * half : 2 * half + 2]:
            for copy in group:
                copy.wait()
        x = x_ref[half * 2 * OWNED : (half + 1) * 2 * OWNED, :]
        both = jnp.dot(x, w_ref[...], preferred_element_type=jnp.float32)
        for k in range(2):
            where = place_of(z, 2 * half + k)
            at = table_rows(where, side)
            mine = slice(k * OWNED, (k + 1) * OWNED)
            out = pl.ds(pl.multiple_of(where * OWNED, OWNED), OWNED)
            kv_ref[out, :HEAD] = rope(both[mine, :HEAD], cos_ref[at, :], sin_ref[at, :]).astype(
                jnp.bfloat16
            )
            kv_ref[out, HEAD:] = both[mine, HEAD:].astype(jnp.bfloat16)


def project_q_kernel(*refs, groups, other):
    count = sum(len(group) for group in groups)
    place_ref = refs[0]
    wq_ref, cos_ref, sin_ref = refs[1 + count : 4 + count]
    q_ref, x_ref, sems = refs[4 + count :]
    z = place_ref[0]
    side = 1 - place_ref[1] if other else place_ref[1]
    copies = start_pieces(refs[1 : 1 + count], groups, x_ref, sems)
    for half in range(2):
        for group in copies[2 * half : 2 * half + 2]:
            for copy in group:
                copy.wait()
        x = x_ref[half * 2 * OWNED : (half + 1) * 2 * OWNED, :]
        query = jnp.dot(x, wq_ref[...], preferred_element_type=jnp.float32)
        for k in range(2):
            where = place_of(z, 2 * half + k)
            at = table_rows(where, side)
            cosine, sine = cos_ref[at, :], sin_ref[at, :]
            mine = slice(k * OWNED, (k + 1) * OWNED)
            for h in range(query.shape[1] // HEAD):
                turned = rope(query[mine, h * HEAD : (h + 1) * HEAD], cosine, sine)
                turned = (turned * SCORE_SCALE).astype(jnp.bfloat16)
                for part in range(PARTS):
                    q_ref[part, where, h] = turned[part * PIECE : (part + 1) * PIECE]


def project(kernel, place, groups, weights, tables, out):
    pieces = [piece for group in groups for piece in group]
    vmem = pl.BlockSpec(memory_space=pltpu.VMEM)
    smem = pl.BlockSpec(memory_space=pltpu.SMEM)
    hbm = pl.BlockSpec(memory_space=pl.ANY)
    width = weights[0].shape[0]
    columns = sum(w.shape[1] for w in weights)
    rows = len(groups) * OWNED
    return pl.pallas_call(
        functools.partial(
            kernel, groups=tuple(tuple(p.shape[0] for p in group) for group in groups)
        ),
        in_specs=[smem] + [hbm] * len(pieces) + [vmem] * (len(weights) + 2),
        out_specs=vmem,
        out_shape=jax.ShapeDtypeStruct(out, jnp.bfloat16),
        scratch_shapes=[
            pltpu.VMEM((rows, width), jnp.bfloat16),
            pltpu.SemaphoreType.DMA((len(pieces),)),
        ],
        compiler_params=pltpu.CompilerParams(vmem_limit_bytes=VMEM_LIMIT),
        cost_estimate=pl.CostEstimate(
            flops=2 * rows * width * columns,
            bytes_accessed=2 * width * (rows + columns),
            transcendentals=0,
        ),
    )(place, *pieces, *weights, *tables)


def start_keys(place_ref, kv_ref, held_ref, sems, n_ctx):
    stride = kv_ref.shape[0] // n_ctx
    copies = []
    for t in range(n_ctx):
        at = pl.multiple_of(lax.rem(place_ref[4] + 1 + t, n_ctx) * stride, 16)
        rows = pl.ds(at, stride)
        copy = pltpu.make_async_copy(kv_ref.at[rows], held_ref.at[rows], sems.at[t])
        copy.start()
        copies.append(copy)
    return copies


def attend_pairs(place_ref, known_ref, kv_ref, held_ref, sems, tiles, heads, far):
    per = 2 * heads * PIECE
    step = 2 * OWNED
    side = place_ref[1]
    n_ctx = sems.shape[0]
    stride = kv_ref.shape[0] // n_ctx
    me = place_ref[4]
    early = (place_ref[2] > place_ref[3]).astype(jnp.int32)
    earliest = jnp.minimum(place_ref[2], place_ref[3])

    def peer(i):
        one, two = known_ref[2 * i], known_ref[2 * i + 1]
        return (one > two).astype(jnp.int32), jnp.minimum(one, two)

    def pair(which, i, half, masked):
        at = pl.multiple_of(i * stride + half * step, 16)
        keys = held_ref[pl.ds(at, step), :HEAD]
        values = held_ref[pl.ds(at, step), HEAD:]
        for other, part, q_ref, max_ref, sum_ref, acc_ref in tiles:
            here = pl.ds(pl.multiple_of(which * per, per), per)
            scores = lax.dot_general(
                q_ref[here, :], keys, (((1,), (1,)), ((), ())),
                preferred_element_type=jnp.float32,
            )
            if masked:
                row = lax.broadcasted_iota(jnp.int32, scores.shape, 0)
                row_side = 1 - side if other else side
                row = (
                    (row // (heads * PIECE)) * (2 * OWNED) + row_side * OWNED
                    + part * PIECE + (row & (PIECE - 1))
                )
                col = lax.broadcasted_iota(jnp.int32, scores.shape, 1)
                col_side = 1 - side if far else side
                col = (col // OWNED) * (2 * OWNED) + col_side * OWNED + (col & (OWNED - 1))
                scores = jnp.where(row >= col, scores, NEGATIVE)
            old = max_ref[here, :]
            new = jnp.maximum(old, jnp.max(scores, axis=1, keepdims=True))
            fade = jnp.exp2(old - new)
            weights = jnp.exp2(scores - jnp.concatenate([new] * (step // HEAD), axis=1))
            if masked:
                weights = jnp.where(row >= col, weights, 0.0)
            max_ref[here, :] = new
            added = weights[:, :HEAD]
            for u in range(1, step // HEAD):
                added = added + weights[:, u * HEAD : (u + 1) * HEAD]
            sum_ref[here, :] = sum_ref[here, :] * fade + added
            acc_ref[here, :] = acc_ref[here, :] * fade + jnp.dot(
                weights.astype(jnp.bfloat16), values, preferred_element_type=jnp.float32
            )

    group = 5 if (n_ctx - 1) % 5 == 0 else 1

    def wait(t):
        rows = pl.ds(0, stride)
        pltpu.make_async_copy(kv_ref.at[rows], held_ref.at[rows], sems.at[t]).wait()

    def body(j, carry):
        for u in range(group):
            wait(j * group + u)
        for u in range(group):
            i = lax.rem(me + 1 + j * group + u, n_ctx)
            lower, least = peer(i)
            pair(1 - early, i, lower, False)
            before = (least < earliest).astype(jnp.int32)
            pair(
                before * early + (1 - before) * (1 - early),
                i, before * lower + (1 - before) * (1 - lower), False,
            )
        return carry

    lax.fori_loop(0, (n_ctx - 1) // group, body, 0)
    wait(n_ctx - 1)
    pair(1 - early, me, early, False)
    for which in range(2):
        pair(which, me, which, True)


def attend_near_kernel(
    place_ref, known_ref, q_near_ref, q_far_ref, kv_ref, *refs, heads, n_ctx
):
    state_refs, (held_ref, sems) = refs[:-2], refs[-2:]
    start_keys(place_ref, kv_ref, held_ref, sems, n_ctx)
    tiles = []
    for index in range(2 * PARTS):
        max_ref, sum_ref, acc_ref = state_refs[3 * index : 3 * index + 3]
        max_ref[...] = jnp.full_like(max_ref, NEGATIVE)
        sum_ref[...] = jnp.zeros_like(sum_ref)
        acc_ref[...] = jnp.zeros_like(acc_ref)
        other, part = index >= PARTS, index % PARTS
        q_ref = (q_far_ref if other else q_near_ref).at[part]
        tiles.append((other, part, q_ref, max_ref, sum_ref, acc_ref))
    attend_pairs(place_ref, known_ref, kv_ref, held_ref, sems, tiles, heads, False)


def attend_far_kernel(
    place_ref, known_ref, q_ref, kv_ref, max_in, sum_in, acc_in, o_ref,
    max_ref, sum_ref, acc_ref, held_ref, sems, *, other, part, heads, n_ctx,
):
    start_keys(place_ref, kv_ref, held_ref, sems, n_ctx)
    max_ref[...] = max_in[...]
    sum_ref[...] = sum_in[...]
    acc_ref[...] = acc_in[...]
    tiles = [(other, part, q_ref, max_ref, sum_ref, acc_ref)]
    attend_pairs(place_ref, known_ref, kv_ref, held_ref, sems, tiles, heads, True)
    for group in range(4):
        for h in range(heads):
            start = (group * heads + h) * PIECE
            here = slice(start, start + PIECE)
            total = jnp.sum(sum_ref[here, :], axis=1, keepdims=True)
            o_ref[group * PIECE : (group + 1) * PIECE, h * HEAD : (h + 1) * HEAD] = (
                acc_ref[here, :] / total
            ).astype(jnp.bfloat16)


def attend_cost(n_ctx, rows, kv):
    scores = (2 * n_ctx + 1) * rows * SPAN // 4
    return pl.CostEstimate(
        flops=scores * HEAD * 8, bytes_accessed=2 * kv.size + 12 * rows * HEAD,
        transcendentals=scores,
    )


def attend_near(place, known, q_near, q_far, kv, heads):
    n_ctx = known.shape[0] // 2
    vmem = pl.BlockSpec(memory_space=pltpu.VMEM)
    smem = pl.BlockSpec(memory_space=pltpu.SMEM)
    return pl.pallas_call(
        functools.partial(attend_near_kernel, heads=heads, n_ctx=n_ctx),
        in_specs=[smem, smem, vmem, vmem, pl.BlockSpec(memory_space=pl.ANY)],
        out_specs=[vmem] * (6 * PARTS),
        out_shape=[jax.ShapeDtypeStruct(q_near.shape[1:], jnp.float32)] * (6 * PARTS),
        scratch_shapes=[
            pltpu.VMEM(kv.shape, jnp.bfloat16), pltpu.SemaphoreType.DMA((n_ctx,)),
        ],
        compiler_params=pltpu.CompilerParams(vmem_limit_bytes=VMEM_LIMIT),
        cost_estimate=attend_cost(n_ctx, 2 * PARTS * q_near.shape[1], kv),
    )(place, known, q_near, q_far, kv)


def attend_far(place, known, query, kv, state, other, part, heads):
    n_ctx = known.shape[0] // 2
    vmem = pl.BlockSpec(memory_space=pltpu.VMEM)
    smem = pl.BlockSpec(memory_space=pltpu.SMEM)
    return pl.pallas_call(
        functools.partial(
            attend_far_kernel, other=other, part=part, heads=heads, n_ctx=n_ctx
        ),
        in_specs=[smem, smem, vmem, pl.BlockSpec(memory_space=pl.ANY)] + [vmem] * 3,
        out_specs=vmem,
        out_shape=jax.ShapeDtypeStruct((4 * PIECE, heads * HEAD), jnp.bfloat16),
        scratch_shapes=[pltpu.VMEM(query.shape, jnp.float32)] * 3 + [
            pltpu.VMEM(kv.shape, jnp.bfloat16), pltpu.SemaphoreType.DMA((n_ctx,)),
        ],
        compiler_params=pltpu.CompilerParams(vmem_limit_bytes=VMEM_LIMIT),
        cost_estimate=attend_cost(n_ctx, query.shape[0], kv),
    )(place, known, query, kv, *state)


def combine_kernel(core_ref, mine_ref, theirs_ref, w_mine_ref, w_own_ref, w_other_ref, out_ref):
    half = theirs_ref.shape[1] // 2
    theirs = theirs_ref[...]
    low = core_ref[0] == 0
    own = jnp.where(low, theirs[:, :half], theirs[:, half:])
    other = jnp.where(low, theirs[:, half:], theirs[:, :half])
    out_ref[...] = (
        jnp.dot(mine_ref[...], w_mine_ref[...], preferred_element_type=jnp.float32)
        + jnp.dot(own, w_own_ref[...], preferred_element_type=jnp.float32)
        + jnp.dot(other, w_other_ref[...], preferred_element_type=jnp.float32)
    ).astype(jnp.bfloat16)


def combine(core, mine, theirs, w_mine, w_own, w_other):
    rows, depth = mine.shape
    columns = w_mine.shape[1]
    step = 1024
    whole = lambda i: (0, 0)
    across = lambda i: (0, i)
    return pl.pallas_call(
        combine_kernel,
        grid=(columns // step,),
        in_specs=[
            pl.BlockSpec(memory_space=pltpu.SMEM),
            pl.BlockSpec((rows, depth), whole),
            pl.BlockSpec((rows, depth), whole),
            pl.BlockSpec((depth, step), across),
            pl.BlockSpec((depth // 2, step), across),
            pl.BlockSpec((depth // 2, step), across),
        ],
        out_specs=pl.BlockSpec((rows, step), across),
        out_shape=jax.ShapeDtypeStruct((rows, columns), jnp.bfloat16),
        compiler_params=pltpu.CompilerParams(vmem_limit_bytes=14 * 2**20),
        cost_estimate=pl.CostEstimate(
            flops=4 * rows * depth * columns,
            bytes_accessed=4 * depth * columns + 2 * rows * columns,
            transcendentals=0,
        ),
    )(core, mine, theirs, w_mine, w_own, w_other)


def per_device(hidden_in, gain, positions, w_query, w_key, w_value, w_out, *, n_ctx):
    ids = positions[::SPAN] // SPAN
    place = jnp.concatenate(
        [
            jnp.stack([lax.axis_index("z"), lax.axis_index("y_hi")]).astype(jnp.int32), ids,
            lax.axis_index(CTX).astype(jnp.int32).reshape(1),
        ]
    )
    widened = hidden_in.astype(jnp.float32)
    scale_rows = lax.rsqrt(jnp.mean(widened * widened, axis=-1, keepdims=True) + EPS)
    normed = (widened * scale_rows * gain.astype(jnp.float32)).astype(jnp.bfloat16)
    across, ahead, behind = lax.optimization_barrier(
        (swap(normed), turn(normed, 1), turn(normed, 3))
    )
    opposite = [turn(ahead[:HALF], 1), turn(behind[HALF:], 3)]
    near = [[normed], [ahead], [behind], opposite]
    crossed = swap(ahead[DIRECT[0] :])
    tables = rope_tables(positions)
    w_kv = jnp.concatenate([w_key, w_value], axis=1)
    core = lax.axis_index("core").astype(jnp.int32)
    half_rows = w_out.shape[0] // 2
    w_own = lax.dynamic_slice_in_dim(w_out, core * half_rows, half_rows, 0)
    near, crossed, w_kv, w_own = lax.optimization_barrier((near, crossed, w_kv, w_own))
    kv_near = project(
        functools.partial(project_kv_kernel, other=False, tail=True),
        place, near, (w_kv,), tables, (4 * OWNED + TAIL, 2 * HEAD),
    )
    kv_near_all = lax.all_gather(kv_near, CTX, axis=0, tiled=True)
    across, near, kv_near = lax.optimization_barrier((across, near, kv_near))
    far = [
        [across],
        [turn(across[: DIRECT[0]], 1), crossed],
        [turn(across[: DIRECT[1]], 3), swap(near[2][0][DIRECT[1] :])],
        [turn(across[: DIRECT[2]], 2), swap(near[3][1][DIRECT[2] - HALF :])],
    ]
    heads = w_query.shape[1] // HEAD

    def queries(groups, other):
        return project(
            functools.partial(project_q_kernel, other=other),
            place, groups, (w_query,), tables, (PARTS, 4, heads, PIECE, HEAD),
        ).reshape(PARTS, 4 * heads * PIECE, HEAD)

    q_near = queries(near, False)
    far, q_near = lax.optimization_barrier((far, q_near))
    kv_far = project(
        functools.partial(project_kv_kernel, other=True, tail=False),
        place, far, (w_kv,), tables, (4 * OWNED, 2 * HEAD),
    )
    kv_near = kv_near_all
    kv_far_all = lax.all_gather(kv_far, CTX, axis=0, tiled=True)
    q_far = queries(far, True)
    kv_far, q_far = lax.optimization_barrier((kv_far, q_far))
    w_own, _ = lax.optimization_barrier((w_own, far))
    w_own = lax.ppermute(w_own, ("y_lo", "y_hi"), [(0, 3), (3, 0), (1, 2), (2, 1)])
    kv_far = kv_far_all
    rows_near = 4 * OWNED + TAIL
    known = kv_near.reshape(n_ctx, rows_near, 2 * HEAD)[:, 4 * OWNED :: TAIL // 2, 0]
    known = known.astype(jnp.int32).reshape(-1)
    state = attend_near(place, known, q_near, q_far, kv_near, heads)
    terms = []
    for part in range(PARTS):
        mine, sent = state[3 * part : 3 * part + 3], state[3 * (PARTS + part) :][:3]
        sent = attend_far(place, known, q_far[part], kv_far, sent, True, part, heads)
        if part == 0:
            sent, w_own = lax.optimization_barrier((sent, w_own))
            w_other = lax.ppermute(w_own, "core", [(0, 1), (1, 0)])
        theirs = swap(sent)
        mine = attend_far(place, known, q_near[part], kv_far, mine, False, part, heads)
        term = combine(core.reshape(1), mine, theirs, w_out, w_own, w_other)
        terms.append(lax.psum_scatter(term, "z", scatter_dimension=0, tiled=True))
    summed = jnp.concatenate(terms, axis=0).astype(jnp.float32)
    return (widened + summed).astype(jnp.bfloat16)


def solution(mesh):
    fine = Mesh(mesh.devices.reshape(2, 4, 2, 4, 2), AXES)
    rows = P(AXES, None)
    tp = AXES[3:]
    in_specs = (rows, P(), P(CTX), P(None, tp), P(None, tp), P(None, tp), P(tp, None))
    return jax.shard_map(
        functools.partial(per_device, n_ctx=mesh.shape["ctx"]),
        mesh=fine, in_specs=in_specs, out_specs=rows, check_vma=False,
    )
```
